256 devices in a mesh: ev: 4 (over z_hi, core), st: 64 (over x, z_lo, y).
Axes of the slice: x: 4, y: 4, z: 8 (z_hi: 2, z_lo: 4; z = z_hi * 4 + z_lo), core: 2. Of those that a mesh axis runs over, the one named last changes fastest.
Arguments:
- waveforms: bfloat16 [192, 512, 384], P('st', 'ev'), may hold values from -160 to 160
- availability: int32 [192, 512], P('st', 'ev'), may hold values 0 or 1
- lag_offset: int32 [192], P('st'), may hold values from -4 to 4
Outputs:
- correlation: float32 [17, 512, 512], P(None, ('ev', 'st'))
The draws below stay inside these ranges and needn't reach their ends.
All inputs are finite; a program needn't handle non-finite values. No bound on the sum of `availability` on one device may be relied on, other than what follows from the above.
Results may differ from the reference program's by a relative error of at most 0.0024.
Values may be sent and summed in bfloat16 or wider, within the bound.
A program may use at most 128 MiB of HBM per device.

```python
import jax
import jax.numpy as jnp
from jax import lax

TS = 128
LAGS = 17
SHIFT_MOST = 4
E = 512
S = 192


def draw_waveforms(key, part):
    keys = jax.random.split(key, 5)
    amplitude = jnp.exp(jax.random.uniform(keys[0], (S, E, 1, 1), jnp.float32, jnp.log(0.3), jnp.log(10.0)))
    gains = jnp.exp(jax.random.uniform(keys[1], (S, E, 3, 1), jnp.float32, jnp.log(0.5), jnp.log(2.0)))
    weights = jax.random.uniform(keys[2], (S, E, 1, 1), jnp.float32, -1.0, 1.0)
    template = jnp.clip(jax.random.normal(keys[3], (S, 1, 3, TS), jnp.float32), -4.0, 4.0)
    noise = jnp.clip(jax.random.normal(keys[4], (S, E, 3, TS), jnp.float32), -4.0, 4.0)
    waves = amplitude * gains * (weights * template + noise)
    return waves.reshape(S, E, 3 * TS).astype(jnp.bfloat16)


def place_ends(result, key, low, largest):
    place = [jax.random.randint(jax.random.fold_in(key, axis), (), 0, length) for axis, length in enumerate(result.shape)]
    widest = result.shape.index(max(result.shape))
    next_to = place[:widest] + [(place[widest] + 1) % result.shape[widest]] + place[widest + 1:]
    return result.at[tuple(place)].set(low).at[tuple(next_to)].set(largest)


def setup_inputs(seed: int = 0) -> dict:
    key_list = jax.random.split(jax.random.key(seed), 4)
    return {
        "waveforms": draw_waveforms(jax.random.fold_in(key_list[3], 71), 0),
        "availability": place_ends((jax.random.randint(key_list[1], (S, E), 0, 5) < 4).astype(jnp.int32), jax.random.fold_in(key_list[1], 1), 0, 1),
        "lag_offset": place_ends(jax.random.randint(key_list[2], (S,), 0 - SHIFT_MOST, SHIFT_MOST + 1), jax.random.fold_in(key_list[2], 1), 0 - SHIFT_MOST, SHIFT_MOST).astype(jnp.int32),
    }


epsilon = 1e-06

def normalize(waveforms, availability):
    wave_float = waveforms.astype(jnp.float32)
    energy = lax.optimization_barrier(jnp.sum(wave_float * wave_float, axis=-1, keepdims=True))
    inverse_norm = availability.astype(jnp.float32)[..., None] * lax.rsqrt(energy + epsilon)
    return (wave_float * inverse_norm).astype(jnp.bfloat16)

def lag_stack(other_rows, shift_now):
    rows_other = other_rows.shape[0]
    samples = other_rows.shape[1] // 3
    pad_reach = SHIFT_MOST + (LAGS - 1) // 2
    split_rows = other_rows.reshape(rows_other, 3, samples)
    padded = jnp.pad(split_rows, ((0, 0), (0, 0), (pad_reach, pad_reach)))
    window = lax.dynamic_slice_in_dim(padded, (SHIFT_MOST + shift_now).astype(jnp.int32), samples + LAGS - 1, 2)
    shifted = jnp.stack([window[:, :, lag_index:lag_index + samples] for lag_index in range(LAGS)], 0)
    return shifted.reshape(LAGS, rows_other, 3 * samples)

def reference(waveforms, availability, lag_offset):
    unit_waves = normalize(waveforms, availability)
    events = unit_waves.shape[1]

    def one_station(totals, inputs):
        own_rows, shift_now = inputs
        shifted = lag_stack(own_rows, shift_now)
        totals = totals + jnp.einsum('ik,ljk->lij', own_rows.astype(jnp.float32), shifted.astype(jnp.float32))
        return (totals, None)
    zero_sums = jnp.zeros((LAGS, events, events), jnp.float32)
    totals, _ = lax.scan(one_station, zero_sums, (unit_waves, lag_offset))
    return totals
```

```python
import functools

import jax
import jax.numpy as jnp
from jax import lax
from jax.experimental import pallas as pl
from jax.experimental.pallas import tpu as pltpu
from jax.sharding import PartitionSpec as P

LAGS = 17
EPSILON = 1e-06
MESH = pl.DeviceIdType.MESH
GROUPS = ((0, 9), (9, 8))
CHUNKS = 4


def place():
    ev, st = lax.axis_index("ev"), lax.axis_index("st")
    return ev, st // 16, (st // 4) % 4, st % 4


def at(ev, x, z, y):
    return (ev, x * 16 + z * 4 + y)


def along(axis, step):
    ev, x, z, y = place()
    if axis == "x":
        return at(ev, (x + step) % 4, z, y)
    if axis == "y":
        return at(ev, x, z, (y + step) % 4)
    return at(ev, x, (z + step) % 4, y)


def kernel(
    offset_ref, wave_ref, avail_ref, out_ref,
    unit, lhs, own, send1, recv1, send2, recv2, send3, recv3,
    gs, gr, ss1, rs1, ss2, rs2, ss3, rs3,
):
    ev, x, z, y = place()
    sibling = at(ev ^ 1, x, z, y)
    partner = at(ev ^ 2, x, z, y)
    stations = wave_ref.shape[0]

    barrier = pltpu.get_barrier_semaphore()
    peers = [along(a, d) for a in "xyz" for d in (1, 2, 3)] + [sibling, partner]
    for peer in peers:
        pl.semaphore_signal(barrier, inc=1, device_id=peer, device_id_type=MESH)

    row = lax.broadcasted_iota(jnp.int32, (128, 128), 0)
    col = lax.broadcasted_iota(jnp.int32, (128, 128), 1)
    for s in range(stations):
        wave = wave_ref[s].astype(jnp.float32)
        energy = jnp.sum(wave * wave, axis=-1, keepdims=True)
        here = avail_ref[pl.ds(s, 1), :].astype(jnp.float32)
        avail = jnp.sum(jnp.where(row == col, here, 0.0), axis=-1, keepdims=True)
        scaled = wave * (avail * lax.rsqrt(energy + EPSILON))
        unit[0, :, s * 384 : (s + 1) * 384] = scaled.astype(jnp.bfloat16)

    a, b, zr = row // 32, (row // 8) % 4, row % 8
    zz, r = zr // 2, zr % 2
    orders = (a * 32 + zz * 8 + b * 2 + r, b * 32 + zz * 8 + a * 2 + r)
    for s in range(stations):
        wave = unit[0, :, s * 384 : (s + 1) * 384]
        for (first, count), order in zip(GROUPS, orders):
            pick = (order == col).astype(jnp.float32).astype(jnp.bfloat16)
            rows = jnp.dot(pick, wave, preferred_element_type=jnp.float32).astype(jnp.bfloat16)
            stack = jnp.concatenate([rows[:, c * 128 : (c + 1) * 128] for c in range(3)], axis=0)
            moves = jnp.concatenate(
                [
                    (col - row == first + k - 8 + offset_ref[s]).astype(jnp.float32).astype(jnp.bfloat16)
                    for k in range(count)
                ],
                axis=1,
            )
            moved = jnp.dot(stack, moves, preferred_element_type=jnp.float32).astype(jnp.bfloat16)
            for k in range(count):
                for c in range(3):
                    lhs[
                        (first + k) * 128 : (first + k + 1) * 128,
                        s * 384 + c * 128 : s * 384 + (c + 1) * 128,
                    ] = moved[c * 128 : (c + 1) * 128, k * 128 : (k + 1) * 128]

    def remote(src, dst, send_sem, recv_sem, target):
        return pltpu.make_async_remote_copy(
            src_ref=src, dst_ref=dst, send_sem=send_sem, recv_sem=recv_sem,
            device_id=target, device_id_type=MESH,
        )

    def multiply(chunk):
        for first, count in GROUPS:
            total = lax.dot_general(
                lhs[first * 128 : (first + count) * 128, :], unit[chunk],
                (((1,), (1,)), ((), ())), preferred_element_type=jnp.float32,
            ).reshape(count, 128, 128)
            own[chunk, first : first + count] = total
            send1[chunk, first : first + count] = total.astype(jnp.bfloat16)

    firsts, seconds = ("x", "y"), ("y", "x")
    index = {"x": x, "y": y, "z": z}

    def stage1(chunk):
        copies = []
        for g, (first, count) in enumerate(GROUPS):
            for d in (1, 2, 3):
                to = (index[firsts[g]] + d) % 4
                copies.append(remote(
                    send1.at[chunk, pl.ds(first, count), pl.ds(pl.multiple_of(to * 32, 32), 32)],
                    recv1.at[chunk, d - 1, pl.ds(first, count)],
                    ss1.at[chunk, g, d - 1], rs1.at[chunk, g, d - 1], along(firsts[g], d),
                ))
        for copy in copies:
            copy.start()
        return copies

    def stage2(chunk, before):
        copies = []
        for g, (first, count) in enumerate(GROUPS):
            for copy in before[3 * g : 3 * g + 3]:
                copy.wait_recv()
            mine = pl.ds(pl.multiple_of(index[firsts[g]] * 32, 32), 32)
            lags = pl.ds(first, count)
            total = own[chunk, lags, mine]
            for d in range(3):
                total = total + recv1[chunk, d, lags].astype(jnp.float32)
            send2[chunk, lags] = total
            for d in (1, 2, 3):
                to = (index[seconds[g]] + d) % 4
                copy = remote(
                    send2.at[chunk, lags, pl.ds(pl.multiple_of(to * 8, 8), 8)],
                    recv2.at[chunk, d - 1, lags],
                    ss2.at[chunk, g, d - 1], rs2.at[chunk, g, d - 1], along(seconds[g], d),
                )
                copy.start()
                copies.append(copy)
        return copies

    def stage3(chunk, before):
        for g, (first, count) in enumerate(GROUPS):
            for copy in before[3 * g : 3 * g + 3]:
                copy.wait_recv()
            mine = pl.ds(pl.multiple_of(index[seconds[g]] * 8, 8), 8)
            lags = pl.ds(first, count)
            total = send2[chunk, lags, mine]
            for d in range(3):
                total = total + recv2[chunk, d, lags]
            for k in range(count):
                for to in range(4):
                    send3[chunk, to, 2 * (first + k) : 2 * (first + k) + 2] = total[k, 2 * to : 2 * to + 2]
        copies = []
        for d in (1, 2, 3):
            copy = remote(
                send3.at[chunk, (z + d) % 4], recv3.at[chunk, d - 1],
                ss3.at[chunk, d - 1], rs3.at[chunk, d - 1], along("z", d),
            )
            copy.start()
            copies.append(copy)
        return copies

    def finish(chunk, before):
        for copy in before:
            copy.wait_recv()
        total = send3[chunk, z]
        for d in range(3):
            total = total + recv3[chunk, d]
        return total

    multiply(0)
    pl.semaphore_wait(barrier, len(peers))

    gather = [
        remote(
            unit.at[0, pl.ds(64 * h, 64)], unit.at[2 + h, pl.ds(0, 64)], gs.at[h], gr.at[h], partner
        )
        for h in range(2)
    ]
    across = remote(unit.at[0], unit.at[1], gs.at[2], gr.at[2], sibling)
    relay = [
        remote(
            unit.at[2 + h, pl.ds(0, 64)], unit.at[2 + h, pl.ds(64, 64)], gs.at[3 + h], gr.at[3 + h], sibling
        )
        for h in range(2)
    ]
    gather[0].start()
    gather[1].start()
    across.start()
    first = [stage1(0)]
    across.wait_recv()
    multiply(1)
    first.append(stage1(1))
    second = [stage2(0, first[0])]
    second.append(stage2(1, first[1]))
    gather[0].wait_recv()
    relay[0].start()
    third = [stage3(0, second[0])]
    relay[0].wait_recv()
    multiply(2)
    first.append(stage1(2))
    third.append(stage3(1, second[1]))
    gather[1].wait_recv()
    relay[1].start()
    second.append(stage2(2, first[2]))
    relay[1].wait_recv()
    multiply(3)
    first.append(stage1(3))
    third.append(stage3(2, second[2]))
    for chunk in range(2):
        block = pl.ds(pl.multiple_of((ev ^ chunk) * 128, 128), 128)
        out_ref[:, block] = finish(chunk, third[chunk])
    second.append(stage2(3, first[3]))
    low = finish(2, third[2])
    third.append(stage3(3, second[3]))
    high = finish(3, third[3])
    left = lax.broadcasted_iota(jnp.int32, low.shape, 1) < 64
    near = pl.ds(pl.multiple_of((ev ^ 2) * 128, 128), 128)
    far = pl.ds(pl.multiple_of((ev ^ 3) * 128, 128), 128)
    out_ref[:, near] = jnp.where(left, low, pltpu.roll(high, 64, 1))
    out_ref[:, far] = jnp.where(left, pltpu.roll(low, 64, 1), high)

    for copy in [*gather, across, *relay]:
        copy.wait_send()
    for group in (first, second, third):
        for copies in group:
            for copy in copies:
                copy.wait_send()


def on_device(waveforms, availability, lag_offset):
    f32, bf16, dma = jnp.float32, jnp.bfloat16, pltpu.SemaphoreType.DMA
    stations, _, width = waveforms.shape
    depth = stations * width
    total = pl.pallas_call(
        kernel,
        out_shape=jax.ShapeDtypeStruct((2 * LAGS, 512), f32),
        in_specs=[
            pl.BlockSpec(memory_space=pltpu.SMEM),
            pl.BlockSpec(memory_space=pltpu.VMEM),
            pl.BlockSpec(memory_space=pltpu.VMEM),
        ],
        out_specs=pl.BlockSpec(memory_space=pltpu.VMEM),
        scratch_shapes=[
            pltpu.VMEM((CHUNKS, 128, depth), bf16),
            pltpu.VMEM((LAGS * 128, depth), bf16),
            pltpu.VMEM((CHUNKS, LAGS, 128, 128), f32),
            pltpu.VMEM((CHUNKS, LAGS, 128, 128), bf16),
            pltpu.VMEM((CHUNKS, 3, LAGS, 32, 128), bf16),
            pltpu.VMEM((CHUNKS, LAGS, 32, 128), f32),
            pltpu.VMEM((CHUNKS, 3, LAGS, 8, 128), f32),
            pltpu.VMEM((CHUNKS, 4, 2 * LAGS, 128), f32),
            pltpu.VMEM((CHUNKS, 3, 2 * LAGS, 128), f32),
            dma((5,)), dma((5,)),
            dma((CHUNKS, 2, 3)), dma((CHUNKS, 2, 3)),
            dma((CHUNKS, 2, 3)), dma((CHUNKS, 2, 3)),
            dma((CHUNKS, 3)), dma((CHUNKS, 3)),
        ],
        compiler_params=pltpu.CompilerParams(
            collective_id=0, has_side_effects=True, vmem_limit_bytes=48 << 20
        ),
    )(lag_offset, waveforms, availability)
    return total.reshape(LAGS, 2, 512)


def solution(mesh):
    placed = (P("st", "ev", None), P("st", "ev"), P("st"))
    return jax.shard_map(
        on_device,
        mesh=mesh,
        in_specs=placed,
        out_specs=P(None, ("ev", "st"), None),
        check_vma=False,
    )
```

```python
import jax
import jax.numpy as jnp
from jax import lax
from jax.experimental import pallas as pl
from jax.experimental.pallas import tpu as pltpu
from jax.sharding import PartitionSpec as P

LAGS = 17
EPSILON = 1e-06
MESH = pl.DeviceIdType.MESH
ORDERS = ((0, 2, 4, 6, 8, 1, 3, 5, 7), (9, 11, 13, 15, 10, 12, 14, 16))
STARTS = (0, 9)
FIRSTS, SECONDS = ("x", "y"), ("y", "x")
CHUNKS = ((0, 128), (128, 128), (256, 128), (384, 64), (448, 64))


def tiles(chunk, group):
    counts = [
        [len(o) if rows == 128 else (len(o) + 1) // 2 for o in ORDERS] for _, rows in CHUNKS
    ]
    first = sum(sum(c) for c in counts[:chunk]) + sum(counts[chunk][:group])
    return first, counts[chunk][group]


def pairs(chunk, group):
    first = sum((tiles(c, g)[1] + 1) // 2 for c in range(chunk) for g in range(2))
    first += sum((tiles(chunk, g)[1] + 1) // 2 for g in range(group))
    return first, (tiles(chunk, group)[1] + 1) // 2


TILES = sum(tiles(c, g)[1] for c in range(len(CHUNKS)) for g in range(2))
PAIRS = sum(pairs(c, g)[1] for c in range(len(CHUNKS)) for g in range(2))


def place():
    ev, st = lax.axis_index("ev"), lax.axis_index("st")
    return ev, st // 16, (st // 4) % 4, st % 4


def at(ev, x, z, y):
    return (ev, x * 16 + z * 4 + y)


def along(axis, step):
    ev, x, z, y = place()
    if axis == "x":
        return at(ev, (x + step) % 4, z, y)
    if axis == "y":
        return at(ev, x, z, (y + step) % 4)
    return at(ev, x, (z + step) % 4, y)


def ones_where(mask):
    return mask.astype(jnp.float32).astype(jnp.bfloat16)


def kernel(
    offset_hbm, wave_hbm, avail_hbm, out_ref,
    offset_ref, wave_ref, avail_ref, unit, lhs, own, send1, recv1, own2, send2, recv2, wide3, wide_in, thin3, thin_in,
    ins, gs, gr, ss1, rs1, ss2, rs2, ss3, rs3,
):
    ev, x, z, y = place()
    index = {"x": x, "y": y, "z": z}
    sibling = at(ev ^ 1, x, z, y)
    partner = at(ev ^ 2, x, z, y)
    stations = wave_ref.shape[0]

    barrier = pltpu.get_barrier_semaphore()
    peers = [along(a, d) for a in "xyz" for d in (1, 2, 3)] + [sibling, partner]
    for peer in peers:
        pl.semaphore_signal(barrier, inc=1, device_id=peer, device_id_type=MESH)

    loads = [
        pltpu.make_async_copy(wave_hbm, wave_ref, ins.at[0]),
        pltpu.make_async_copy(avail_hbm, avail_ref, ins.at[1]),
        pltpu.make_async_copy(offset_hbm, offset_ref, ins.at[2]),
    ]
    for load in loads:
        load.start()
    for load in loads:
        load.wait()

    row = lax.broadcasted_iota(jnp.int32, (128, 128), 0)
    col = lax.broadcasted_iota(jnp.int32, (128, 128), 1)
    for s in range(stations):
        wave = wave_ref[s].astype(jnp.float32)
        energy = jnp.sum(wave * wave, axis=-1, keepdims=True)
        here = avail_ref[pl.ds(s, 1), :].astype(jnp.float32)
        avail = jnp.sum(jnp.where(row == col, here, 0.0), axis=-1, keepdims=True)
        scaled = wave * (avail * lax.rsqrt(energy + EPSILON))
        unit[0:128, s * 384 : (s + 1) * 384] = scaled.astype(jnp.bfloat16)

    def remote(src, dst, send_sem, recv_sem, target):
        return pltpu.make_async_remote_copy(
            src_ref=src, dst_ref=dst, send_sem=send_sem, recv_sem=recv_sem,
            device_id=target, device_id_type=MESH,
        )

    pl.semaphore_wait(barrier, len(peers))

    parts = ((0, 64, 256), (64, 32, 384), (96, 32, 448))
    gather = [
        remote(unit.at[pl.ds(low, n)], unit.at[pl.ds(to, n)], gs.at[h], gr.at[h], partner)
        for h, (low, n, to) in enumerate(parts)
    ]
    across = remote(unit.at[pl.ds(0, 128)], unit.at[pl.ds(128, 128)], gs.at[3], gr.at[3], sibling)
    relay = [
        remote(unit.at[pl.ds(to, n)], unit.at[pl.ds(to + n, n)], gs.at[4 + h], gr.at[4 + h], sibling)
        for h, (_, n, to) in enumerate(parts)
    ]

    for copy in gather:
        copy.start()
    across.start()

    a, b, zr = row // 32, (row // 8) % 4, row % 8
    zz, r = zr // 2, zr % 2
    places = (a * 32 + zz * 8 + b * 2 + r, b * 32 + zz * 8 + a * 2 + r)
    for s in range(stations):
        wave = unit[0:128, s * 384 : (s + 1) * 384]
        for start, order, source in zip(STARTS, ORDERS, places):
            rows = jnp.dot(ones_where(source == col), wave, preferred_element_type=jnp.float32).astype(jnp.bfloat16)
            stack = jnp.concatenate([rows[:, c * 128 : (c + 1) * 128] for c in range(3)], axis=0)
            moves = jnp.concatenate([ones_where(col - row == lag - 8 + offset_ref[s]) for lag in order], axis=1)
            moved = jnp.dot(stack, moves, preferred_element_type=jnp.float32).astype(jnp.bfloat16)
            for k in range(len(order)):
                for c in range(3):
                    lhs[
                        (start + k) * 128 : (start + k + 1) * 128,
                        s * 384 + c * 128 : s * 384 + (c + 1) * 128,
                    ] = moved[c * 128 : (c + 1) * 128, k * 128 : (k + 1) * 128]

    def multiply(chunk, group):
        at_row, rows = CHUNKS[chunk]
        first, count = tiles(chunk, group)
        start, order = STARTS[group], ORDERS[group]

        def dot(low, high):
            return lax.dot_general(
                lhs[(start + low) * 128 : (start + high) * 128, :], unit[at_row : at_row + rows, :],
                (((1,), (1,)), ((), ())), preferred_element_type=jnp.float32,
            )

        if rows == 128:
            total = dot(0, count)
        else:
            left, right = dot(0, count), dot(count, len(order))
            if len(order) % 2:
                right = jnp.concatenate([right, jnp.zeros((128, rows), jnp.float32)], axis=0)
            total = jnp.concatenate([left, right], axis=1)
        total = total.reshape(count, 128, 128)
        own[first : first + count] = total
        send1[first : first + count] = total.astype(jnp.bfloat16)

    def copies1(chunk, group):
        first, count = tiles(chunk, group)
        some = pl.ds(first, count)
        axis = FIRSTS[group]
        return [
            remote(
                send1.at[some, pl.ds(pl.multiple_of((index[axis] + d) % 4 * 32, 32), 32)],
                recv1.at[d - 1, some],
                ss1.at[chunk, group, d - 1], rs1.at[chunk, group, d - 1], along(axis, d),
            )
            for d in (2, 1, 3)
        ]

    def stage1(chunk):
        copies = [None, None]
        for group in range(2):
            multiply(chunk, group)
            copies[group] = copies1(chunk, group)
            for copy in copies[group]:
                copy.start()
        return copies

    def stage2(chunk, before):
        copies = [None, None]
        for group in range(2):
            for copy in before[group]:
                copy.wait_recv()
            first, count = tiles(chunk, group)
            pair, half = pairs(chunk, group)
            total = own[first : first + count, pl.ds(pl.multiple_of(index[FIRSTS[group]] * 32, 32), 32)]
            for d in range(3):
                total = total + recv1[d, first : first + count].astype(jnp.float32)
            own2[first : first + count] = total
            for p in range(half):
                one, two = total[2 * p], total[min(2 * p + 1, count - 1)]
                for to in range(4):
                    both = jnp.concatenate([one[8 * to : 8 * to + 8], two[8 * to : 8 * to + 8]], axis=0)
                    send2[to, pair + p] = both.astype(jnp.bfloat16)
            axis = SECONDS[group]
            copies[group] = [
                remote(
                    send2.at[(index[axis] + d) % 4, pl.ds(pair, half)], recv2.at[d - 1, pl.ds(pair, half)],
                    ss2.at[chunk, group, d - 1], rs2.at[chunk, group, d - 1], along(axis, d),
                )
                for d in (2, 1, 3)
            ]
            for copy in copies[group]:
                copy.start()
        return copies

    def buffers3(chunk):
        return (wide3.at[chunk], wide_in.at[chunk]) if chunk < 3 else (thin3.at[chunk - 3], thin_in.at[chunk - 3])

    def stage3(chunk, before):
        out3, in3 = buffers3(chunk)
        base = tiles(chunk, 0)[0]
        for group in range(2):
            for copy in before[group]:
                copy.wait_recv()
            first, count = tiles(chunk, group)
            pair, half = pairs(chunk, group)
            mine = own2[first : first + count, pl.ds(pl.multiple_of(index[SECONDS[group]] * 8, 8), 8)]
            others = recv2[0, pair : pair + half].astype(jnp.float32)
            for d in (1, 2):
                others = others + recv2[d, pair : pair + half].astype(jnp.float32)
            for k in range(count):
                total = mine[k] + others[k // 2, k % 2 * 8 : k % 2 * 8 + 8]
                place3 = 2 * (ORDERS[group][k] if chunk < 3 else first + k - base)
                for to in range(4):
                    out3[to, place3 : place3 + 2] = total[2 * to : 2 * to + 2]
        copies = [
            remote(
                out3.at[(z + d) % 4], in3.at[d - 1],
                ss3.at[chunk, d - 1], rs3.at[chunk, d - 1], along("z", d),
            )
            for d in (2, 1, 3)
        ]
        for copy in copies:
            copy.start()
        return copies

    def finish(chunk, before):
        out3, in3 = buffers3(chunk)
        for copy in before:
            copy.wait_recv()
        total = out3[z]
        for d in range(3):
            total = total + in3[d]
        if chunk < 3:
            return total
        halves = (total, pltpu.roll(total, 64, 1))
        rows = []
        for lag in range(LAGS):
            group = 0 if lag in ORDERS[0] else 1
            first, count = tiles(chunk, group)
            k = ORDERS[group].index(lag)
            at_row = 2 * (first - tiles(chunk, 0)[0] + k % count)
            rows.append(halves[k // count][at_row : at_row + 2])
        return jnp.concatenate(rows, axis=0)

    def pass_on(h):
        gather[h].wait_recv()
        relay[h].start()

    first, second, third = {}, {}, {}
    first[0] = stage1(0)
    across.wait_recv()
    first[1] = stage1(1)
    second[0] = stage2(0, first[0])
    pass_on(0)
    relay[0].wait_recv()
    first[2] = stage1(2)
    second[1] = stage2(1, first[1])
    pass_on(1)
    relay[1].wait_recv()
    first[3] = stage1(3)
    pass_on(2)
    relay[2].wait_recv()
    first[4] = stage1(4)
    for chunk in (0, 1):
        third[chunk] = stage3(chunk, second[chunk])
    for chunk in (2, 3, 4):
        second[chunk] = stage2(chunk, first[chunk])
    for chunk in (2, 3, 4):
        third[chunk] = stage3(chunk, second[chunk])
    for chunk in range(2):
        block = pl.ds(pl.multiple_of((ev ^ chunk) * 128, 128), 128)
        out_ref[:, block] = finish(chunk, third[chunk])
    half, quarter, last = (finish(chunk, third[chunk]) for chunk in (2, 3, 4))
    lane = lax.broadcasted_iota(jnp.int32, half.shape, 1)
    near = pl.ds(pl.multiple_of((ev ^ 2) * 128, 128), 128)
    far = pl.ds(pl.multiple_of((ev ^ 3) * 128, 128), 128)
    out_ref[:, near] = jnp.where(
        lane < 64, half, jnp.where(lane < 96, pltpu.roll(quarter, 64, 1), pltpu.roll(last, 96, 1))
    )
    out_ref[:, far] = jnp.where(
        lane < 64, pltpu.roll(half, 64, 1),
        jnp.where(lane < 96, pltpu.roll(quarter, 32, 1), pltpu.roll(last, 64, 1)),
    )

    for copy in [*gather, across, *relay]:
        copy.wait_send()
    for chunk in range(len(CHUNKS)):
        for copy in [*first[chunk][0], *first[chunk][1], *second[chunk][0], *second[chunk][1], *third[chunk]]:
            copy.wait_send()


def on_device(waveforms, availability, lag_offset):
    f32, bf16, dma = jnp.float32, jnp.bfloat16, pltpu.SemaphoreType.DMA
    stations, _, width = waveforms.shape
    depth = stations * width
    chunks = len(CHUNKS)
    total = pl.pallas_call(
        kernel,
        out_shape=pltpu.VMEM((2 * LAGS, 512), f32),
        in_specs=[pl.BlockSpec(memory_space=pltpu.HBM)] * 3,
        out_specs=pl.BlockSpec(memory_space=pltpu.VMEM),
        scratch_shapes=[
            pltpu.SMEM(lag_offset.shape, jnp.int32),
            pltpu.VMEM(waveforms.shape, bf16),
            pltpu.VMEM(availability.shape, jnp.int32),
            pltpu.VMEM((512, depth), bf16),
            pltpu.VMEM((LAGS * 128, depth), bf16),
            pltpu.VMEM((TILES, 128, 128), f32),
            pltpu.VMEM((TILES, 128, 128), bf16),
            pltpu.VMEM((3, TILES, 32, 128), bf16),
            pltpu.VMEM((TILES, 32, 128), f32),
            pltpu.VMEM((4, PAIRS, 16, 128), bf16),
            pltpu.VMEM((3, PAIRS, 16, 128), bf16),
            pltpu.VMEM((3, 4, 2 * LAGS, 128), f32),
            pltpu.VMEM((3, 3, 2 * LAGS, 128), f32),
            pltpu.VMEM((2, 4, LAGS + 1, 128), f32),
            pltpu.VMEM((2, 3, LAGS + 1, 128), f32),
            dma((3,)),
            dma((7,)), dma((7,)),
            dma((chunks, 2, 3)), dma((chunks, 2, 3)),
            dma((chunks, 2, 3)), dma((chunks, 2, 3)),
            dma((chunks, 3)), dma((chunks, 3)),
        ],
        compiler_params=pltpu.CompilerParams(
            collective_id=0, has_side_effects=True, vmem_limit_bytes=60 << 20
        ),
    )(lag_offset, waveforms, availability)
    return total.reshape(LAGS, 2, 512)


def solution(mesh):
    placed = (P("st", "ev", None), P("st", "ev"), P("st"))
    return jax.shard_map(
        on_device,
        mesh=mesh,
        in_specs=placed,
        out_specs=P(None, ("ev", "st"), None),
        check_vma=False,
    )
```

```python
import jax
import jax.numpy as jnp
from jax import lax
from jax.experimental import pallas as pl
from jax.experimental.pallas import tpu as pltpu
from jax.sharding import PartitionSpec as P

LAGS = 17
EPSILON = 1e-06
MESH = pl.DeviceIdType.MESH
ORDERS = ((8, 0, 2, 4, 6, 1, 3, 5, 7), (8, 9, 11, 13, 15, 10, 12, 14, 16))
DEPTH = len(ORDERS[0])
FIRSTS, SECONDS = ("x", "y"), ("y", "x")
CHUNKS = ((0, 128), (128, 128), (256, 128), (384, 64), (448, 64))


def lags(chunk, group):
    return ORDERS[group][(chunk + group) % 2 :]


def tiles(chunk, group):
    counts = [
        [len(lags(c, g)) if rows == 128 else (len(lags(c, g)) + 1) // 2 for g in range(2)]
        for c, (_, rows) in enumerate(CHUNKS)
    ]
    first = sum(sum(c) for c in counts[:chunk]) + sum(counts[chunk][:group])
    return first, counts[chunk][group]


def pairs(chunk, group):
    first = sum((tiles(c, g)[1] + 1) // 2 for c in range(chunk) for g in range(2))
    first += sum((tiles(chunk, g)[1] + 1) // 2 for g in range(group))
    return first, (tiles(chunk, group)[1] + 1) // 2


TILES = sum(tiles(c, g)[1] for c in range(len(CHUNKS)) for g in range(2))
PAIRS = sum(pairs(c, g)[1] for c in range(len(CHUNKS)) for g in range(2))


def place():
    ev, st = lax.axis_index("ev"), lax.axis_index("st")
    return ev, st // 16, (st // 4) % 4, st % 4


def at(ev, x, z, y):
    return (ev, x * 16 + z * 4 + y)


def along(axis, step):
    ev, x, z, y = place()
    if axis == "x":
        return at(ev, (x + step) % 4, z, y)
    if axis == "y":
        return at(ev, x, z, (y + step) % 4)
    return at(ev, x, (z + step) % 4, y)


def ones_where(mask):
    return mask.astype(jnp.float32).astype(jnp.bfloat16)


def kernel(
    offset_hbm, wave_hbm, avail_hbm, out_ref,
    offset_ref, wave_ref, avail_ref, unit, lhs, own, send1, recv1, own2, send2, recv2, wide3, wide_in, thin3, thin_in,
    ins, gs, gr, ss1, rs1, ss2, rs2, ss3, rs3,
):
    ev, x, z, y = place()
    index = {"x": x, "y": y, "z": z}
    sibling = at(ev ^ 1, x, z, y)
    partner = at(ev ^ 2, x, z, y)
    stations = wave_ref.shape[0]

    barrier = pltpu.get_barrier_semaphore()
    peers = [along(a, d) for a in "xyz" for d in (1, 2, 3)] + [sibling, partner]
    for peer in peers:
        pl.semaphore_signal(barrier, inc=1, device_id=peer, device_id_type=MESH)

    loads = [
        pltpu.make_async_copy(wave_hbm, wave_ref, ins.at[0]),
        pltpu.make_async_copy(avail_hbm, avail_ref, ins.at[1]),
        pltpu.make_async_copy(offset_hbm, offset_ref, ins.at[2]),
    ]
    for load in loads:
        load.start()
    for load in loads:
        load.wait()

    row = lax.broadcasted_iota(jnp.int32, (128, 128), 0)
    col = lax.broadcasted_iota(jnp.int32, (128, 128), 1)
    for s in range(stations):
        wave = wave_ref[s].astype(jnp.float32)
        energy = jnp.sum(wave * wave, axis=-1, keepdims=True)
        here = avail_ref[pl.ds(s, 1), :].astype(jnp.float32)
        avail = jnp.sum(jnp.where(row == col, here, 0.0), axis=-1, keepdims=True)
        scaled = wave * (avail * lax.rsqrt(energy + EPSILON))
        unit[0:128, s * 384 : (s + 1) * 384] = scaled.astype(jnp.bfloat16)

    def remote(src, dst, send_sem, recv_sem, target):
        return pltpu.make_async_remote_copy(
            src_ref=src, dst_ref=dst, send_sem=send_sem, recv_sem=recv_sem,
            device_id=target, device_id_type=MESH,
        )

    pl.semaphore_wait(barrier, len(peers))

    parts = ((0, 64, 256), (64, 32, 384), (96, 32, 448))
    gather = [
        remote(unit.at[pl.ds(low, n)], unit.at[pl.ds(to, n)], gs.at[h], gr.at[h], partner)
        for h, (low, n, to) in enumerate(parts)
    ]
    across = remote(unit.at[pl.ds(0, 128)], unit.at[pl.ds(128, 128)], gs.at[3], gr.at[3], sibling)
    relay = [
        remote(unit.at[pl.ds(to, n)], unit.at[pl.ds(to + n, n)], gs.at[4 + h], gr.at[4 + h], sibling)
        for h, (_, n, to) in enumerate(parts)
    ]

    gather[0].start()
    across.start()

    a, b, zr = row // 32, (row // 8) % 4, row % 8
    zz, r = zr // 2, zr % 2
    places = (a * 32 + zz * 8 + b * 2 + r, b * 32 + zz * 8 + a * 2 + r)

    def shift_rows(group):
        order, source, start = ORDERS[group], places[group], DEPTH * group
        for s in range(stations):
            wave = unit[0:128, s * 384 : (s + 1) * 384]
            rows = jnp.dot(ones_where(source == col), wave, preferred_element_type=jnp.float32).astype(jnp.bfloat16)
            stack = jnp.concatenate([rows[:, c * 128 : (c + 1) * 128] for c in range(3)], axis=0)
            moves = jnp.concatenate([ones_where(col - row == lag - 8 + offset_ref[s]) for lag in order], axis=1)
            moved = jnp.dot(stack, moves, preferred_element_type=jnp.float32).astype(jnp.bfloat16)
            for k in range(len(order)):
                for c in range(3):
                    lhs[
                        (start + k) * 128 : (start + k + 1) * 128,
                        s * 384 + c * 128 : s * 384 + (c + 1) * 128,
                    ] = moved[c * 128 : (c + 1) * 128, k * 128 : (k + 1) * 128]

    def multiply(chunk, group):
        at_row, rows = CHUNKS[chunk]
        first, count = tiles(chunk, group)
        order = lags(chunk, group)
        start = DEPTH * (group + 1) - len(order)

        def dot(low, high):
            return lax.dot_general(
                lhs[(start + low) * 128 : (start + high) * 128, :], unit[at_row : at_row + rows, :],
                (((1,), (1,)), ((), ())), preferred_element_type=jnp.float32,
            )

        if rows == 128:
            total = dot(0, count)
        else:
            left, right = dot(0, count), dot(count, len(order))
            if len(order) % 2:
                right = jnp.concatenate([right, jnp.zeros((128, rows), jnp.float32)], axis=0)
            total = jnp.concatenate([left, right], axis=1)
        total = total.reshape(count, 128, 128)
        own[first : first + count] = total
        send1[first : first + count] = total.astype(jnp.bfloat16)

    def multiply_own(group):
        total = lax.dot_general(
            lhs[DEPTH * group * 128 : DEPTH * (group + 1) * 128, :], unit[0:256, :],
            (((1,), (1,)), ((), ())), preferred_element_type=jnp.float32,
        )
        for chunk in range(2):
            first, count = tiles(chunk, group)
            some = total[(DEPTH - count) * 128 :, chunk * 128 : (chunk + 1) * 128].reshape(count, 128, 128)
            own[first : first + count] = some
            send1[first : first + count] = some.astype(jnp.bfloat16)

    def copies1(chunk, group):
        first, count = tiles(chunk, group)
        some = pl.ds(first, count)
        axis = FIRSTS[group]
        return [
            remote(
                send1.at[some, pl.ds(pl.multiple_of((index[axis] + d) % 4 * 32, 32), 32)],
                recv1.at[d - 1, some],
                ss1.at[chunk, group, d - 1], rs1.at[chunk, group, d - 1], along(axis, d),
            )
            for d in (2, 1, 3)
        ]

    def stage1(chunk):
        copies = [None, None]
        for group in range(2):
            multiply(chunk, group)
            copies[group] = copies1(chunk, group)
            for copy in copies[group]:
                copy.start()
        return copies

    def stage2(chunk, before):
        copies = [None, None]
        for group in range(2):
            for copy in before[group]:
                copy.wait_recv()
            first, count = tiles(chunk, group)
            pair, half = pairs(chunk, group)
            total = own[first : first + count, pl.ds(pl.multiple_of(index[FIRSTS[group]] * 32, 32), 32)]
            for d in range(3):
                total = total + recv1[d, first : first + count].astype(jnp.float32)
            own2[first : first + count] = total
            for p in range(half):
                one, two = total[2 * p], total[min(2 * p + 1, count - 1)]
                for to in range(4):
                    both = jnp.concatenate([one[8 * to : 8 * to + 8], two[8 * to : 8 * to + 8]], axis=0)
                    send2[to, pair + p] = both.astype(jnp.bfloat16)
            axis = SECONDS[group]
            copies[group] = [
                remote(
                    send2.at[(index[axis] + d) % 4, pl.ds(pair, half)], recv2.at[d - 1, pl.ds(pair, half)],
                    ss2.at[chunk, group, d - 1], rs2.at[chunk, group, d - 1], along(axis, d),
                )
                for d in (2, 1, 3)
            ]
            for copy in copies[group]:
                copy.start()
        return copies

    def buffers3(chunk):
        return (wide3.at[chunk], wide_in.at[chunk]) if chunk < 3 else (thin3.at[chunk - 3], thin_in.at[chunk - 3])

    def stage3(chunk, before):
        out3, in3 = buffers3(chunk)
        base = tiles(chunk, 0)[0]
        for group in range(2):
            for copy in before[group]:
                copy.wait_recv()
            first, count = tiles(chunk, group)
            pair, half = pairs(chunk, group)
            mine = own2[first : first + count, pl.ds(pl.multiple_of(index[SECONDS[group]] * 8, 8), 8)]
            others = recv2[0, pair : pair + half].astype(jnp.float32)
            for d in (1, 2):
                others = others + recv2[d, pair : pair + half].astype(jnp.float32)
            for k in range(count):
                total = mine[k] + others[k // 2, k % 2 * 8 : k % 2 * 8 + 8]
                place3 = 2 * (lags(chunk, group)[k] if chunk < 3 else first + k - base)
                for to in range(4):
                    out3[to, place3 : place3 + 2] = total[2 * to : 2 * to + 2]
        copies = [
            remote(
                out3.at[(z + d) % 4], in3.at[d - 1],
                ss3.at[chunk, d - 1], rs3.at[chunk, d - 1], along("z", d),
            )
            for d in (2, 1, 3)
        ]
        for copy in copies:
            copy.start()
        return copies

    def finish(chunk, before):
        out3, in3 = buffers3(chunk)
        for copy in before:
            copy.wait_recv()
        total = out3[z]
        for d in range(3):
            total = total + in3[d]
        if chunk < 3:
            return total
        halves = (total, pltpu.roll(total, 64, 1))
        rows = []
        for lag in range(LAGS):
            group = 0 if lag in lags(chunk, 0) else 1
            first, count = tiles(chunk, group)
            k = lags(chunk, group).index(lag)
            at_row = 2 * (first - tiles(chunk, 0)[0] + k % count)
            rows.append(halves[k // count][at_row : at_row + 2])
        return jnp.concatenate(rows, axis=0)

    def pass_on(h):
        gather[h].wait_recv()
        relay[h].start()

    first, second, third = {}, {}, {}
    first[0], first[1] = [None, None], [None, None]
    for group in range(2):
        shift_rows(group)
        if group == 0:
            across.wait_recv()
        multiply_own(group)
        for chunk in range(2):
            first[chunk][group] = copies1(chunk, group)
            for copy in first[chunk][group]:
                copy.start()
    gather[0].wait_send()
    gather[1].start()
    pass_on(0)
    gather[1].wait_send()
    gather[2].start()
    relay[0].wait_recv()
    first[2] = stage1(2)
    second[0] = stage2(0, first[0])
    pass_on(1)
    relay[1].wait_recv()
    first[3] = stage1(3)
    second[1] = stage2(1, first[1])
    pass_on(2)
    relay[2].wait_recv()
    first[4] = stage1(4)
    second[2] = stage2(2, first[2])
    second[3] = stage2(3, first[3])
    third[0] = stage3(0, second[0])
    third[1] = stage3(1, second[1])
    second[4] = stage2(4, first[4])
    third[2] = stage3(2, second[2])
    third[3] = stage3(3, second[3])
    third[4] = stage3(4, second[4])
    for chunk in range(2):
        block = pl.ds(pl.multiple_of((ev ^ chunk) * 128, 128), 128)
        out_ref[:, block] = finish(chunk, third[chunk])
    half, quarter, last = (finish(chunk, third[chunk]) for chunk in (2, 3, 4))
    lane = lax.broadcasted_iota(jnp.int32, half.shape, 1)
    near = pl.ds(pl.multiple_of((ev ^ 2) * 128, 128), 128)
    far = pl.ds(pl.multiple_of((ev ^ 3) * 128, 128), 128)
    out_ref[:, near] = jnp.where(
        lane < 64, half, jnp.where(lane < 96, pltpu.roll(quarter, 64, 1), pltpu.roll(last, 96, 1))
    )
    out_ref[:, far] = jnp.where(
        lane < 64, pltpu.roll(half, 64, 1),
        jnp.where(lane < 96, pltpu.roll(quarter, 32, 1), pltpu.roll(last, 64, 1)),
    )

    for copy in [gather[2], across, *relay]:
        copy.wait_send()
    for chunk in range(len(CHUNKS)):
        for copy in [*first[chunk][0], *first[chunk][1], *second[chunk][0], *second[chunk][1], *third[chunk]]:
            copy.wait_send()


def on_device(waveforms, availability, lag_offset):
    f32, bf16, dma = jnp.float32, jnp.bfloat16, pltpu.SemaphoreType.DMA
    stations, _, width = waveforms.shape
    depth = stations * width
    chunks = len(CHUNKS)
    total = pl.pallas_call(
        kernel,
        out_shape=pltpu.VMEM((2 * LAGS, 512), f32),
        in_specs=[pl.BlockSpec(memory_space=pltpu.HBM)] * 3,
        out_specs=pl.BlockSpec(memory_space=pltpu.VMEM),
        scratch_shapes=[
            pltpu.SMEM(lag_offset.shape, jnp.int32),
            pltpu.VMEM(waveforms.shape, bf16),
            pltpu.VMEM(availability.shape, jnp.int32),
            pltpu.VMEM((512, depth), bf16),
            pltpu.VMEM((2 * DEPTH * 128, depth), bf16),
            pltpu.VMEM((TILES, 128, 128), f32),
            pltpu.VMEM((TILES, 128, 128), bf16),
            pltpu.VMEM((3, TILES, 32, 128), bf16),
            pltpu.VMEM((TILES, 32, 128), f32),
            pltpu.VMEM((4, PAIRS, 16, 128), bf16),
            pltpu.VMEM((3, PAIRS, 16, 128), bf16),
            pltpu.VMEM((3, 4, 2 * LAGS, 128), f32),
            pltpu.VMEM((3, 3, 2 * LAGS, 128), f32),
            pltpu.VMEM((2, 4, LAGS + 1, 128), f32),
            pltpu.VMEM((2, 3, LAGS + 1, 128), f32),
            dma((3,)),
            dma((7,)), dma((7,)),
            dma((chunks, 2, 3)), dma((chunks, 2, 3)),
            dma((chunks, 2, 3)), dma((chunks, 2, 3)),
            dma((chunks, 3)), dma((chunks, 3)),
        ],
        compiler_params=pltpu.CompilerParams(
            collective_id=0, has_side_effects=True, vmem_limit_bytes=60 << 20
        ),
    )(lag_offset, waveforms, availability)
    return total.reshape(LAGS, 2, 512)


def solution(mesh):
    placed = (P("st", "ev", None), P("st", "ev"), P("st"))
    return jax.shard_map(
        on_device,
        mesh=mesh,
        in_specs=placed,
        out_specs=P(None, ("ev", "st"), None),
        check_vma=False,
    )
```

```python
import jax
import jax.numpy as jnp
from jax import lax
from jax.experimental import pallas as pl
from jax.experimental.pallas import tpu as pltpu
from jax.sharding import PartitionSpec as P

LAGS = 17
EPSILON = 1e-06
MESH = pl.DeviceIdType.MESH
ORDERS = ((8, 0, 2, 4, 6, 1, 3, 5, 7), (8, 9, 11, 13, 15, 10, 12, 14, 16))
DEPTH = len(ORDERS[0])
FIRSTS, SECONDS = ("x", "y"), ("y", "x")
CHUNKS = ((0, 128), (128, 128), (256, 128), (384, 64), (448, 64))


def lags(chunk, group):
    return ORDERS[group][(chunk + group) % 2 :]


def tiles(chunk, group):
    counts = [
        [len(lags(c, g)) if rows == 128 else (len(lags(c, g)) + 1) // 2 for g in range(2)]
        for c, (_, rows) in enumerate(CHUNKS)
    ]
    first = sum(sum(c) for c in counts[:chunk]) + sum(counts[chunk][:group])
    return first, counts[chunk][group]


def pairs(chunk, group):
    first = sum((tiles(c, g)[1] + 1) // 2 for c in range(chunk) for g in range(2))
    first += sum((tiles(chunk, g)[1] + 1) // 2 for g in range(group))
    return first, (tiles(chunk, group)[1] + 1) // 2


TILES = sum(tiles(c, g)[1] for c in range(len(CHUNKS)) for g in range(2))
PAIRS = sum(pairs(c, g)[1] for c in range(len(CHUNKS)) for g in range(2))


def place():
    ev, st = lax.axis_index("ev"), lax.axis_index("st")
    return ev, st // 16, (st // 4) % 4, st % 4


def at(ev, x, z, y):
    return (ev, x * 16 + z * 4 + y)


def along(axis, step):
    ev, x, z, y = place()
    if axis == "x":
        return at(ev, (x + step) % 4, z, y)
    if axis == "y":
        return at(ev, x, z, (y + step) % 4)
    return at(ev, x, (z + step) % 4, y)


def ones_where(mask):
    return mask.astype(jnp.float32).astype(jnp.bfloat16)


def kernel(
    offset_hbm, wave_hbm, avail_hbm, out_ref,
    offset_ref, wave_ref, avail_ref, unit, lhs, own, send1, recv1, own2, send2, recv2, wide3, wide_in, thin3, thin_in,
    ins, gs, gr, ss1, rs1, ss2, rs2, ss3, rs3,
):
    ev, x, z, y = place()
    index = {"x": x, "y": y, "z": z}
    sibling = at(ev ^ 1, x, z, y)
    partner = at(ev ^ 2, x, z, y)
    stations = wave_ref.shape[0]

    barrier = pltpu.get_barrier_semaphore()
    peers = [partner] + [along(a, d) for a in "zxy" for d in (1, 2, 3)] + [sibling]
    for peer in peers:
        pl.semaphore_signal(barrier, inc=1, device_id=peer, device_id_type=MESH)

    loads = [
        pltpu.make_async_copy(wave_hbm, wave_ref, ins.at[0]),
        pltpu.make_async_copy(avail_hbm, avail_ref, ins.at[1]),
        pltpu.make_async_copy(offset_hbm, offset_ref, ins.at[2]),
    ]
    for load in loads:
        load.start()
    for load in loads:
        load.wait()

    row = lax.broadcasted_iota(jnp.int32, (128, 128), 0)
    col = lax.broadcasted_iota(jnp.int32, (128, 128), 1)
    for s in range(stations):
        wave = wave_ref[s].astype(jnp.float32)
        energy = jnp.sum(wave * wave, axis=-1, keepdims=True)
        here = avail_ref[pl.ds(s, 1), :].astype(jnp.float32)
        avail = jnp.sum(jnp.where(row == col, here, 0.0), axis=-1, keepdims=True)
        scaled = wave * (avail * lax.rsqrt(energy + EPSILON))
        unit[0:128, s * 384 : (s + 1) * 384] = scaled.astype(jnp.bfloat16)

    def remote(src, dst, send_sem, recv_sem, target):
        return pltpu.make_async_remote_copy(
            src_ref=src, dst_ref=dst, send_sem=send_sem, recv_sem=recv_sem,
            device_id=target, device_id_type=MESH,
        )

    pl.semaphore_wait(barrier, len(peers))

    parts = ((0, 64, 256), (64, 32, 384), (96, 32, 448))
    gather = [
        remote(unit.at[pl.ds(low, n)], unit.at[pl.ds(to, n)], gs.at[h], gr.at[h], partner)
        for h, (low, n, to) in enumerate(parts)
    ]
    across = remote(unit.at[pl.ds(0, 128)], unit.at[pl.ds(128, 128)], gs.at[3], gr.at[3], sibling)
    relay = [
        remote(unit.at[pl.ds(to, n)], unit.at[pl.ds(to + n, n)], gs.at[4 + h], gr.at[4 + h], sibling)
        for h, (_, n, to) in enumerate(parts)
    ]

    gather[0].start()
    across.start()

    a, b, zr = row // 32, (row // 8) % 4, row % 8
    zz, r = zr // 2, zr % 2
    places = (a * 32 + zz * 8 + b * 2 + r, b * 32 + zz * 8 + a * 2 + r)

    def shift_rows(group):
        order, source, start = ORDERS[group], places[group], DEPTH * group
        for s in range(stations):
            wave = unit[0:128, s * 384 : (s + 1) * 384]
            rows = jnp.dot(ones_where(source == col), wave, preferred_element_type=jnp.float32).astype(jnp.bfloat16)
            stack = jnp.concatenate([rows[:, c * 128 : (c + 1) * 128] for c in range(3)], axis=0)
            moves = jnp.concatenate([ones_where(col - row == lag - 8 + offset_ref[s]) for lag in order], axis=1)
            moved = jnp.dot(stack, moves, preferred_element_type=jnp.float32).astype(jnp.bfloat16)
            for k in range(len(order)):
                for c in range(3):
                    lhs[
                        (start + k) * 128 : (start + k + 1) * 128,
                        s * 384 + c * 128 : s * 384 + (c + 1) * 128,
                    ] = moved[c * 128 : (c + 1) * 128, k * 128 : (k + 1) * 128]

    def multiply(chunk, group):
        at_row, rows = CHUNKS[chunk]
        first, count = tiles(chunk, group)
        order = lags(chunk, group)
        start = DEPTH * (group + 1) - len(order)

        def dot(low, high):
            return lax.dot_general(
                lhs[(start + low) * 128 : (start + high) * 128, :], unit[at_row : at_row + rows, :],
                (((1,), (1,)), ((), ())), preferred_element_type=jnp.float32,
            )

        if rows == 128:
            total = dot(0, count)
        else:
            left, right = dot(0, count), dot(count, len(order))
            if len(order) % 2:
                right = jnp.concatenate([right, jnp.zeros((128, rows), jnp.float32)], axis=0)
            total = jnp.concatenate([left, right], axis=1)
        total = total.reshape(count, 128, 128)
        own[first : first + count] = total
        send1[first : first + count] = total.astype(jnp.bfloat16)

    def multiply_own(group):
        total = lax.dot_general(
            lhs[DEPTH * group * 128 : DEPTH * (group + 1) * 128, :], unit[0:256, :],
            (((1,), (1,)), ((), ())), preferred_element_type=jnp.float32,
        )
        for chunk in range(2):
            first, count = tiles(chunk, group)
            some = total[(DEPTH - count) * 128 :, chunk * 128 : (chunk + 1) * 128].reshape(count, 128, 128)
            own[first : first + count] = some
            send1[first : first + count] = some.astype(jnp.bfloat16)

    def copies1(chunk, group):
        first, count = tiles(chunk, group)
        some = pl.ds(first, count)
        axis = FIRSTS[group]
        return [
            remote(
                send1.at[some, pl.ds(pl.multiple_of((index[axis] + d) % 4 * 32, 32), 32)],
                recv1.at[d - 1, some],
                ss1.at[chunk, group, d - 1], rs1.at[chunk, group, d - 1], along(axis, d),
            )
            for d in (2, 1, 3)
        ]

    def stage1(chunk):
        copies = [None, None]
        for group in range(2):
            multiply(chunk, group)
            copies[group] = copies1(chunk, group)
            for copy in copies[group]:
                copy.start()
        return copies

    def stage2(chunk, before):
        copies = [None, None]
        for group in range(2):
            for copy in before[group]:
                copy.wait_recv()
            first, count = tiles(chunk, group)
            pair, half = pairs(chunk, group)
            total = own[first : first + count, pl.ds(pl.multiple_of(index[FIRSTS[group]] * 32, 32), 32)]
            for d in range(3):
                total = total + recv1[d, first : first + count].astype(jnp.float32)
            own2[first : first + count] = total
            for p in range(half):
                one, two = total[2 * p], total[min(2 * p + 1, count - 1)]
                for to in range(4):
                    both = jnp.concatenate([one[8 * to : 8 * to + 8], two[8 * to : 8 * to + 8]], axis=0)
                    send2[to, pair + p] = both.astype(jnp.bfloat16)
            axis = SECONDS[group]
            copies[group] = [
                remote(
                    send2.at[(index[axis] + d) % 4, pl.ds(pair, half)], recv2.at[d - 1, pl.ds(pair, half)],
                    ss2.at[chunk, group, d - 1], rs2.at[chunk, group, d - 1], along(axis, d),
                )
                for d in (2, 1, 3)
            ]
            for copy in copies[group]:
                copy.start()
        return copies

    def buffers3(chunk):
        return (wide3.at[chunk], wide_in.at[chunk]) if chunk < 3 else (thin3.at[chunk - 3], thin_in.at[chunk - 3])

    def stage3(chunk, before):
        out3, in3 = buffers3(chunk)
        base = tiles(chunk, 0)[0]
        for group in range(2):
            for copy in before[group]:
                copy.wait_recv()
            first, count = tiles(chunk, group)
            pair, half = pairs(chunk, group)
            mine = own2[first : first + count, pl.ds(pl.multiple_of(index[SECONDS[group]] * 8, 8), 8)]
            others = recv2[0, pair : pair + half].astype(jnp.float32)
            for d in (1, 2):
                others = others + recv2[d, pair : pair + half].astype(jnp.float32)
            for k in range(count):
                total = mine[k] + others[k // 2, k % 2 * 8 : k % 2 * 8 + 8]
                place3 = 2 * (lags(chunk, group)[k] if chunk < 3 else first + k - base)
                for to in range(4):
                    out3[to, place3 : place3 + 2] = total[2 * to : 2 * to + 2]
        copies = [
            remote(
                out3.at[(z + d) % 4], in3.at[d - 1],
                ss3.at[chunk, d - 1], rs3.at[chunk, d - 1], along("z", d),
            )
            for d in (2, 1, 3)
        ]
        for copy in copies:
            copy.start()
        return copies

    def finish(chunk, before):
        out3, in3 = buffers3(chunk)
        for copy in before:
            copy.wait_recv()
        total = out3[z]
        for d in range(3):
            total = total + in3[d]
        if chunk < 3:
            return total
        halves = (total, pltpu.roll(total, 64, 1))
        rows = []
        for lag in range(LAGS):
            group = 0 if lag in lags(chunk, 0) else 1
            first, count = tiles(chunk, group)
            k = lags(chunk, group).index(lag)
            at_row = 2 * (first - tiles(chunk, 0)[0] + k % count)
            rows.append(halves[k // count][at_row : at_row + 2])
        return jnp.concatenate(rows, axis=0)

    def pass_on(h):
        gather[h].wait_recv()
        relay[h].start()

    first, second, third = {}, {}, {}
    first[0], first[1] = [None, None], [None, None]
    for group in range(2):
        shift_rows(group)
        if group == 0:
            across.wait_recv()
        multiply_own(group)
        for chunk in range(2):
            first[chunk][group] = copies1(chunk, group)
            for copy in first[chunk][group]:
                copy.start()
    gather[0].wait_send()
    gather[1].start()
    pass_on(0)
    gather[1].wait_send()
    gather[2].start()
    relay[0].wait_recv()
    first[2] = stage1(2)
    second[0] = stage2(0, first[0])
    pass_on(1)
    relay[1].wait_recv()
    first[3] = stage1(3)
    second[1] = stage2(1, first[1])
    pass_on(2)
    relay[2].wait_recv()
    first[4] = stage1(4)
    second[2] = stage2(2, first[2])
    second[3] = stage2(3, first[3])
    third[0] = stage3(0, second[0])
    third[1] = stage3(1, second[1])
    second[4] = stage2(4, first[4])
    third[2] = stage3(2, second[2])
    third[3] = stage3(3, second[3])
    third[4] = stage3(4, second[4])
    for copy in [gather[2], across, *relay]:
        copy.wait_send()
    for chunk in range(len(CHUNKS)):
        for copy in [*first[chunk][0], *first[chunk][1], *second[chunk][0], *second[chunk][1]]:
            copy.wait_send()
    for chunk in range(len(CHUNKS) - 1):
        for copy in third[chunk]:
            copy.wait_send()
    for chunk in range(2):
        block = pl.ds(pl.multiple_of((ev ^ chunk) * 128, 128), 128)
        out_ref[:, block] = finish(chunk, third[chunk])
    half, quarter, last = (finish(chunk, third[chunk]) for chunk in (2, 3, 4))
    lane = lax.broadcasted_iota(jnp.int32, half.shape, 1)
    near = pl.ds(pl.multiple_of((ev ^ 2) * 128, 128), 128)
    far = pl.ds(pl.multiple_of((ev ^ 3) * 128, 128), 128)
    out_ref[:, near] = jnp.where(
        lane < 64, half, jnp.where(lane < 96, pltpu.roll(quarter, 64, 1), pltpu.roll(last, 96, 1))
    )
    out_ref[:, far] = jnp.where(
        lane < 64, pltpu.roll(half, 64, 1),
        jnp.where(lane < 96, pltpu.roll(quarter, 32, 1), pltpu.roll(last, 64, 1)),
    )

    for copy in third[len(CHUNKS) - 1]:
        copy.wait_send()


def on_device(waveforms, availability, lag_offset):
    f32, bf16, dma = jnp.float32, jnp.bfloat16, pltpu.SemaphoreType.DMA
    stations, _, width = waveforms.shape
    depth = stations * width
    chunks = len(CHUNKS)
    total = pl.pallas_call(
        kernel,
        out_shape=pltpu.VMEM((2 * LAGS, 512), f32),
        in_specs=[pl.BlockSpec(memory_space=pltpu.HBM)] * 3,
        out_specs=pl.BlockSpec(memory_space=pltpu.VMEM),
        scratch_shapes=[
            pltpu.SMEM(lag_offset.shape, jnp.int32),
            pltpu.VMEM(waveforms.shape, bf16),
            pltpu.VMEM(availability.shape, jnp.int32),
            pltpu.VMEM((512, depth), bf16),
            pltpu.VMEM((2 * DEPTH * 128, depth), bf16),
            pltpu.VMEM((TILES, 128, 128), f32),
            pltpu.VMEM((TILES, 128, 128), bf16),
            pltpu.VMEM((3, TILES, 32, 128), bf16),
            pltpu.VMEM((TILES, 32, 128), f32),
            pltpu.VMEM((4, PAIRS, 16, 128), bf16),
            pltpu.VMEM((3, PAIRS, 16, 128), bf16),
            pltpu.VMEM((3, 4, 2 * LAGS, 128), f32),
            pltpu.VMEM((3, 3, 2 * LAGS, 128), f32),
            pltpu.VMEM((2, 4, LAGS + 1, 128), f32),
            pltpu.VMEM((2, 3, LAGS + 1, 128), f32),
            dma((3,)),
            dma((7,)), dma((7,)),
            dma((chunks, 2, 3)), dma((chunks, 2, 3)),
            dma((chunks, 2, 3)), dma((chunks, 2, 3)),
            dma((chunks, 3)), dma((chunks, 3)),
        ],
        compiler_params=pltpu.CompilerParams(
            collective_id=0, has_side_effects=True, vmem_limit_bytes=60 << 20
        ),
    )(lag_offset, waveforms, availability)
    return total.reshape(LAGS, 2, 512)


def solution(mesh):
    placed = (P("st", "ev", None), P("st", "ev"), P("st"))
    return jax.shard_map(
        on_device,
        mesh=mesh,
        in_specs=placed,
        out_specs=P(None, ("ev", "st"), None),
        check_vma=False,
    )
```

```python
import jax
import jax.numpy as jnp
from jax import lax
from jax.experimental import pallas as pl
from jax.experimental.pallas import tpu as pltpu
from jax.sharding import PartitionSpec as P

LAGS = 17
EPSILON = 1e-06
MESH = pl.DeviceIdType.MESH
ORDERS = ((8, 0, 2, 4, 6, 1, 3, 5, 7), (8, 9, 11, 13, 15, 10, 12, 14, 16))
DEPTH = len(ORDERS[0])
FIRSTS, SECONDS = ("x", "y"), ("y", "x")
CHUNKS = ((0, 128), (128, 128), (256, 128), (384, 64), (448, 64))


def lags(chunk, group):
    return ORDERS[group][(chunk + group) % 2 :]


def tiles(chunk, group):
    counts = [
        [len(lags(c, g)) if rows == 128 else (len(lags(c, g)) + 1) // 2 for g in range(2)]
        for c, (_, rows) in enumerate(CHUNKS)
    ]
    first = sum(sum(c) for c in counts[:chunk]) + sum(counts[chunk][:group])
    return first, counts[chunk][group]


def pairs(chunk, group):
    first = sum((tiles(c, g)[1] + 1) // 2 for c in range(chunk) for g in range(2))
    first += sum((tiles(chunk, g)[1] + 1) // 2 for g in range(group))
    return first, (tiles(chunk, group)[1] + 1) // 2


TILES = sum(tiles(c, g)[1] for c in range(len(CHUNKS)) for g in range(2))
PAIRS = sum(pairs(c, g)[1] for c in range(len(CHUNKS)) for g in range(2))


def place():
    ev, st = lax.axis_index("ev"), lax.axis_index("st")
    return ev, st // 16, (st // 4) % 4, st % 4


def at(ev, x, z, y):
    return (ev, x * 16 + z * 4 + y)


def along(axis, step):
    ev, x, z, y = place()
    if axis == "x":
        return at(ev, (x + step) % 4, z, y)
    if axis == "y":
        return at(ev, x, z, (y + step) % 4)
    return at(ev, x, (z + step) % 4, y)


def ones_where(mask):
    return mask.astype(jnp.float32).astype(jnp.bfloat16)


def kernel(
    offset_hbm, wave_hbm, avail_hbm, out_ref,
    offset_ref, wave_ref, avail_ref, unit, lhs, own, send1, recv1, own2, send2, recv2, wide3, wide_in, thin3, thin_in,
    ins, gs, gr, ss1, rs1, ss2, rs2, ss3, rs3,
):
    ev, x, z, y = place()
    index = {"x": x, "y": y, "z": z}
    sibling = at(ev ^ 1, x, z, y)
    partner = at(ev ^ 2, x, z, y)
    stations = wave_ref.shape[0]

    barrier = pltpu.get_barrier_semaphore()
    peers = [partner] + [along(a, d) for a in "zxy" for d in (1, 2, 3)] + [sibling]
    for peer in peers:
        pl.semaphore_signal(barrier, inc=1, device_id=peer, device_id_type=MESH)

    loads = [
        pltpu.make_async_copy(wave_hbm, wave_ref, ins.at[0]),
        pltpu.make_async_copy(avail_hbm, avail_ref, ins.at[1]),
        pltpu.make_async_copy(offset_hbm, offset_ref, ins.at[2]),
    ]
    for load in loads:
        load.start()
    for load in loads:
        load.wait()

    row = lax.broadcasted_iota(jnp.int32, (128, 128), 0)
    col = lax.broadcasted_iota(jnp.int32, (128, 128), 1)
    for s in range(stations):
        wave = wave_ref[s].astype(jnp.float32)
        energy = jnp.sum(wave * wave, axis=-1, keepdims=True)
        here = avail_ref[pl.ds(s, 1), :].astype(jnp.float32)
        avail = jnp.sum(jnp.where(row == col, here, 0.0), axis=-1, keepdims=True)
        scaled = wave * (avail * lax.rsqrt(energy + EPSILON))
        unit[0:128, s * 384 : (s + 1) * 384] = scaled.astype(jnp.bfloat16)

    def remote(src, dst, send_sem, recv_sem, target):
        return pltpu.make_async_remote_copy(
            src_ref=src, dst_ref=dst, send_sem=send_sem, recv_sem=recv_sem,
            device_id=target, device_id_type=MESH,
        )

    pl.semaphore_wait(barrier, len(peers))

    parts = ((0, 64, 256), (64, 32, 384), (96, 32, 448))
    gather = [
        remote(unit.at[pl.ds(low, n)], unit.at[pl.ds(to, n)], gs.at[h], gr.at[h], partner)
        for h, (low, n, to) in enumerate(parts)
    ]
    across = remote(unit.at[pl.ds(0, 128)], unit.at[pl.ds(128, 128)], gs.at[3], gr.at[3], sibling)
    relay = [
        remote(unit.at[pl.ds(to, n)], unit.at[pl.ds(to + n, n)], gs.at[4 + h], gr.at[4 + h], sibling)
        for h, (_, n, to) in enumerate(parts)
    ]

    gather[0].start()
    across.start()

    a, b, zr = row // 32, (row // 8) % 4, row % 8
    zz, r = zr // 2, zr % 2
    places = (a * 32 + zz * 8 + b * 2 + r, b * 32 + zz * 8 + a * 2 + r)

    def shift_rows(group):
        order, source, start = ORDERS[group], places[group], DEPTH * group
        for s in range(stations):
            wave = unit[0:128, s * 384 : (s + 1) * 384]
            rows = jnp.dot(ones_where(source == col), wave, preferred_element_type=jnp.float32).astype(jnp.bfloat16)
            stack = jnp.concatenate([rows[:, c * 128 : (c + 1) * 128] for c in range(3)], axis=0)
            moves = jnp.concatenate([ones_where(col - row == lag - 8 + offset_ref[s]) for lag in order], axis=1)
            moved = jnp.dot(stack, moves, preferred_element_type=jnp.float32).astype(jnp.bfloat16)
            for k in range(len(order)):
                for c in range(3):
                    lhs[
                        (start + k) * 128 : (start + k + 1) * 128,
                        s * 384 + c * 128 : s * 384 + (c + 1) * 128,
                    ] = moved[c * 128 : (c + 1) * 128, k * 128 : (k + 1) * 128]

    def multiply(chunk, group):
        at_row, rows = CHUNKS[chunk]
        first, count = tiles(chunk, group)
        order = lags(chunk, group)
        start = DEPTH * (group + 1) - len(order)

        def dot(low, high):
            return lax.dot_general(
                lhs[(start + low) * 128 : (start + high) * 128, :], unit[at_row : at_row + rows, :],
                (((1,), (1,)), ((), ())), preferred_element_type=jnp.float32,
            )

        if rows == 128:
            total = dot(0, count)
        else:
            left, right = dot(0, count), dot(count, len(order))
            if len(order) % 2:
                right = jnp.concatenate([right, jnp.zeros((128, rows), jnp.float32)], axis=0)
            total = jnp.concatenate([left, right], axis=1)
        total = total.reshape(count, 128, 128)
        own[first : first + count] = total
        send1[first : first + count] = total.astype(jnp.bfloat16)

    def multiply_own(group):
        total = lax.dot_general(
            lhs[DEPTH * group * 128 : DEPTH * (group + 1) * 128, :], unit[0:256, :],
            (((1,), (1,)), ((), ())), preferred_element_type=jnp.float32,
        )
        for chunk in range(2):
            first, count = tiles(chunk, group)
            some = total[(DEPTH - count) * 128 :, chunk * 128 : (chunk + 1) * 128].reshape(count, 128, 128)
            own[first : first + count] = some
            send1[first : first + count] = some.astype(jnp.bfloat16)

    def copies1(chunk, group):
        first, count = tiles(chunk, group)
        some = pl.ds(first, count)
        axis = FIRSTS[group]
        return [
            remote(
                send1.at[some, pl.ds(pl.multiple_of((index[axis] + d) % 4 * 32, 32), 32)],
                recv1.at[d - 1, some],
                ss1.at[chunk, group, d - 1], rs1.at[chunk, group, d - 1], along(axis, d),
            )
            for d in (2, 1, 3)
        ]

    def stage1(chunk):
        copies = [None, None]
        for group in range(2):
            multiply(chunk, group)
            copies[group] = copies1(chunk, group)
            for copy in copies[group]:
                copy.start()
        return copies

    def stage2(chunk, before):
        copies = [None, None]
        for group in range(2):
            for copy in before[group]:
                copy.wait_recv()
            first, count = tiles(chunk, group)
            pair, half = pairs(chunk, group)
            total = own[first : first + count, pl.ds(pl.multiple_of(index[FIRSTS[group]] * 32, 32), 32)]
            for d in range(3):
                total = total + recv1[d, first : first + count].astype(jnp.float32)
            own2[first : first + count] = total
            for p in range(half):
                one, two = total[2 * p], total[min(2 * p + 1, count - 1)]
                for to in range(4):
                    both = jnp.concatenate([one[8 * to : 8 * to + 8], two[8 * to : 8 * to + 8]], axis=0)
                    send2[to, pair + p] = both.astype(jnp.bfloat16)
            axis = SECONDS[group]
            copies[group] = [
                remote(
                    send2.at[(index[axis] + d) % 4, pl.ds(pair, half)], recv2.at[d - 1, pl.ds(pair, half)],
                    ss2.at[chunk, group, d - 1], rs2.at[chunk, group, d - 1], along(axis, d),
                )
                for d in (2, 1, 3)
            ]
            for copy in copies[group]:
                copy.start()
        return copies

    def buffers3(chunk):
        return (wide3.at[chunk], wide_in.at[chunk]) if chunk < 3 else (thin3.at[chunk - 3], thin_in.at[chunk - 3])

    def stage3(chunk, before):
        out3, in3 = buffers3(chunk)
        base = tiles(chunk, 0)[0]
        for group in range(2):
            for copy in before[group]:
                copy.wait_recv()
            first, count = tiles(chunk, group)
            pair, half = pairs(chunk, group)
            mine = own2[first : first + count, pl.ds(pl.multiple_of(index[SECONDS[group]] * 8, 8), 8)]
            others = recv2[0, pair : pair + half].astype(jnp.float32)
            for d in (1, 2):
                others = others + recv2[d, pair : pair + half].astype(jnp.float32)
            for k in range(count):
                total = mine[k] + others[k // 2, k % 2 * 8 : k % 2 * 8 + 8]
                place3 = 2 * (lags(chunk, group)[k] if chunk < 3 else first + k - base)
                for to in range(4):
                    out3[to, place3 : place3 + 2] = total[2 * to : 2 * to + 2]
        copies = [
            remote(
                out3.at[(z + d) % 4], in3.at[d - 1],
                ss3.at[chunk, d - 1], rs3.at[chunk, d - 1], along("z", d),
            )
            for d in (2, 1, 3)
        ]
        for copy in copies:
            copy.start()
        return copies

    def finish(chunk, before):
        out3, in3 = buffers3(chunk)
        for copy in before:
            copy.wait_recv()
        total = out3[z]
        for d in range(3):
            total = total + in3[d]
        if chunk < 3:
            return total
        halves = (total, pltpu.roll(total, 64, 1))
        rows = []
        for lag in range(LAGS):
            group = 0 if lag in lags(chunk, 0) else 1
            first, count = tiles(chunk, group)
            k = lags(chunk, group).index(lag)
            at_row = 2 * (first - tiles(chunk, 0)[0] + k % count)
            rows.append(halves[k // count][at_row : at_row + 2])
        return jnp.concatenate(rows, axis=0)

    def pass_on(h):
        gather[h].wait_recv()
        relay[h].start()

    first, second, third = {}, {}, {}
    first[0], first[1] = [None, None], [None, None]
    for group in range(2):
        shift_rows(group)
        if group == 0:
            across.wait_recv()
        multiply_own(group)
        for chunk in range(2):
            first[chunk][group] = copies1(chunk, group)
            for copy in first[chunk][group]:
                copy.start()
    gather[0].wait_send()
    gather[1].start()
    pass_on(0)
    gather[1].wait_send()
    gather[2].start()
    relay[0].wait_recv()
    first[2] = stage1(2)
    pass_on(1)
    second[0] = stage2(0, first[0])
    relay[1].wait_recv()
    first[3] = stage1(3)
    pass_on(2)
    second[1] = stage2(1, first[1])
    relay[2].wait_recv()
    first[4] = stage1(4)
    second[2] = stage2(2, first[2])
    second[3] = stage2(3, first[3])
    third[0] = stage3(0, second[0])
    third[1] = stage3(1, second[1])
    second[4] = stage2(4, first[4])
    third[2] = stage3(2, second[2])
    third[3] = stage3(3, second[3])
    third[4] = stage3(4, second[4])
    for copy in [gather[2], across, *relay]:
        copy.wait_send()
    for chunk in range(len(CHUNKS)):
        for copy in [*first[chunk][0], *first[chunk][1], *second[chunk][0], *second[chunk][1]]:
            copy.wait_send()
    for chunk in range(len(CHUNKS) - 1):
        for copy in third[chunk]:
            copy.wait_send()
    for chunk in range(2):
        block = pl.ds(pl.multiple_of((ev ^ chunk) * 128, 128), 128)
        out_ref[:, block] = finish(chunk, third[chunk])
    half, quarter, last = (finish(chunk, third[chunk]) for chunk in (2, 3, 4))
    lane = lax.broadcasted_iota(jnp.int32, half.shape, 1)
    near = pl.ds(pl.multiple_of((ev ^ 2) * 128, 128), 128)
    far = pl.ds(pl.multiple_of((ev ^ 3) * 128, 128), 128)
    out_ref[:, near] = jnp.where(
        lane < 64, half, jnp.where(lane < 96, pltpu.roll(quarter, 64, 1), pltpu.roll(last, 96, 1))
    )
    out_ref[:, far] = jnp.where(
        lane < 64, pltpu.roll(half, 64, 1),
        jnp.where(lane < 96, pltpu.roll(quarter, 32, 1), pltpu.roll(last, 64, 1)),
    )

    for copy in third[len(CHUNKS) - 1]:
        copy.wait_send()


def on_device(waveforms, availability, lag_offset):
    f32, bf16, dma = jnp.float32, jnp.bfloat16, pltpu.SemaphoreType.DMA
    stations, _, width = waveforms.shape
    depth = stations * width
    chunks = len(CHUNKS)
    total = pl.pallas_call(
        kernel,
        out_shape=pltpu.VMEM((2 * LAGS, 512), f32),
        in_specs=[pl.BlockSpec(memory_space=pltpu.HBM)] * 3,
        out_specs=pl.BlockSpec(memory_space=pltpu.VMEM),
        scratch_shapes=[
            pltpu.SMEM(lag_offset.shape, jnp.int32),
            pltpu.VMEM(waveforms.shape, bf16),
            pltpu.VMEM(availability.shape, jnp.int32),
            pltpu.VMEM((512, depth), bf16),
            pltpu.VMEM((2 * DEPTH * 128, depth), bf16),
            pltpu.VMEM((TILES, 128, 128), f32),
            pltpu.VMEM((TILES, 128, 128), bf16),
            pltpu.VMEM((3, TILES, 32, 128), bf16),
            pltpu.VMEM((TILES, 32, 128), f32),
            pltpu.VMEM((4, PAIRS, 16, 128), bf16),
            pltpu.VMEM((3, PAIRS, 16, 128), bf16),
            pltpu.VMEM((3, 4, 2 * LAGS, 128), f32),
            pltpu.VMEM((3, 3, 2 * LAGS, 128), f32),
            pltpu.VMEM((2, 4, LAGS + 1, 128), f32),
            pltpu.VMEM((2, 3, LAGS + 1, 128), f32),
            dma((3,)),
            dma((7,)), dma((7,)),
            dma((chunks, 2, 3)), dma((chunks, 2, 3)),
            dma((chunks, 2, 3)), dma((chunks, 2, 3)),
            dma((chunks, 3)), dma((chunks, 3)),
        ],
        compiler_params=pltpu.CompilerParams(
            collective_id=0, has_side_effects=True, vmem_limit_bytes=60 << 20
        ),
    )(lag_offset, waveforms, availability)
    return total.reshape(LAGS, 2, 512)


def solution(mesh):
    placed = (P("st", "ev", None), P("st", "ev"), P("st"))
    return jax.shard_map(
        on_device,
        mesh=mesh,
        in_specs=placed,
        out_specs=P(None, ("ev", "st"), None),
        check_vma=False,
    )
```
